256 devices in a mesh: outer: 16 (over y, x_hi, core), inner: 16 (over z, x_lo).
Axes of the slice: x: 4 (x_hi: 2, x_lo: 2; x = x_hi * 2 + x_lo), y: 4, z: 8, core: 2. Of those that a mesh axis runs over, the one named last changes fastest.
Arguments:
- queries: bfloat16 [6144, 8192], P('inner', 'outer'), may hold values from -6 to 6
- keys_values: bfloat16 [6144, 2048], P('inner', 'outer'), may hold values from -18 to 18
- stretch_ids: int32 [32], P('inner'), may hold values from 0 to 31, each once
- d_out: bfloat16 [6144, 8192], P('inner', 'outer'), may hold values from -6 to 6
Outputs:
- attn_out: bfloat16 [6144, 8192], P('inner', 'outer')
- d_query: bfloat16 [6144, 8192], P('inner', 'outer')
- d_keys_values: bfloat16 [6144, 2048], P('inner', 'outer')
The draws below stay inside these ranges and needn't reach their ends.
Inputs may be any that keep to these rules, and one draw needn't show every extreme that they name: `stretch_ids`: every number of 0 to 31 appears exactly once.
All inputs are finite; a program needn't handle non-finite values.
Results may differ from the reference program's by a relative error of at most 0.024.
Values may be sent and summed in bfloat16 or wider, within the bound.
No kernel may reach another device: no remote copies, remote signals or barrier semaphores. Data moves between devices by JAX's collectives and lax.ppermute only.
A program may use at most 64 MiB of HBM per device.

```python
import math
import jax
import jax.numpy as jnp
from jax import lax

H = 4
DH = 128
STRETCH = 192
STRETCHES = 32
TOKENS = 6144
QHEADS = 64
KVHEADS = 8


def draw_queries(key, part):
    key = jax.random.fold_in(key, 5)
    base_rows = jnp.clip(jax.random.normal(key, (TOKENS, QHEADS * DH), jnp.float32), -6.0, 6.0)
    return base_rows.astype(jnp.bfloat16)


def draw_keys_values(key, part):
    key = jax.random.fold_in(key, 9)
    key_row, key_col, key_base, key_value = jax.random.split(key, 4)
    row_scale = jnp.exp(jax.random.uniform(key_row, (TOKENS, KVHEADS, 1), jnp.float32, math.log(0.3), math.log(3.0)))
    col_scale = jnp.exp(jax.random.uniform(key_col, (1, KVHEADS, DH), jnp.float32, math.log(0.5), math.log(2.0)))
    base_rows = jnp.clip(jax.random.normal(key_base, (TOKENS, KVHEADS, DH), jnp.float32), -3.0, 3.0)
    values = jnp.clip(jax.random.normal(key_value, (TOKENS, KVHEADS, DH), jnp.float32), -4.0, 4.0)
    key_rows = base_rows * row_scale * col_scale
    stacked = jnp.stack([key_rows, values], 2)
    return stacked.reshape(TOKENS, 2 * KVHEADS * DH).astype(jnp.bfloat16)


def steps_of(rng, shape, cuts, low, high):
    def one(dim, parts):
        heights = jax.random.uniform(jax.random.fold_in(jax.random.fold_in(rng, 6), dim), (parts,), jnp.float32, low / len(cuts), high / len(cuts))
        return jnp.repeat(jnp.exp(heights), shape[dim] // parts).reshape((-1,) + (1,) * (len(shape) - dim - 1))

    gain = one(*cuts[0])
    for cut in cuts[1:]:
        gain = gain * one(*cut)
    return gain


def noise(stream_key, dims, deviation, limit, cuts=(), held_as=jnp.bfloat16):
    loudness = steps_of(stream_key, dims, cuts, -0.22, 0.18) if cuts else 1.0
    values = jax.random.normal(stream_key, dims, jnp.float32) * deviation * loudness
    return jnp.minimum(jnp.maximum(values, -limit), limit).astype(held_as)


def setup_inputs(seed: int = 0) -> dict:
    key_list = jax.random.split(jax.random.key(seed), 5)
    queries = draw_queries(jax.random.fold_in(key_list[4], 71), 0)
    keys_values = draw_keys_values(jax.random.fold_in(key_list[4], 71), 0)
    stretch_ids = jax.random.permutation(key_list[2], STRETCHES).astype(jnp.int32)
    d_out = noise(key_list[3], (TOKENS, QHEADS * DH), 1.0, 6.0, ((0, 16), (1, 16)))
    return {"queries": queries, "keys_values": keys_values, "stretch_ids": stretch_ids, "d_out": d_out}


def attend(query_rows, grad_rows, key_rows, value_rows, heads):
    block_rows = min(512, TOKENS)
    block_count = TOKENS // block_rows
    scaling = DH ** (-0.5)
    span_rows = block_rows * heads

    def block_scores(query_block, key_block):
        query_part = lax.dynamic_slice_in_dim(query_rows, query_block * span_rows, span_rows)
        key_part = lax.dynamic_slice_in_dim(key_rows, key_block * block_rows, block_rows)
        scores = jnp.dot(query_part.astype(jnp.float32), key_part.astype(jnp.float32).T, preferred_element_type=jnp.float32) * scaling
        query_pos = query_block * block_rows + jnp.arange(span_rows, dtype=jnp.int32) // heads
        key_pos = key_block * block_rows + jnp.arange(block_rows, dtype=jnp.int32)
        admitted = key_pos[None, :] <= query_pos[:, None]
        return (scores, admitted)

    def forward(query_block):

        def statistics(key_block, running):
            maxima, totals = running
            scores, admitted = block_scores(query_block, key_block)
            scores = jnp.where(admitted, scores, -1e+30)
            new_max = jnp.maximum(maxima, scores.max(1))
            totals = totals * jnp.exp(maxima - new_max) + lax.optimization_barrier(jnp.sum(jnp.where(admitted, jnp.exp(scores - new_max[:, None]), 0.0), 1))
            return (new_max, totals)
        initial = (jnp.full((span_rows,), -1e+30, jnp.float32), jnp.zeros((span_rows,), jnp.float32))
        maxima, totals = lax.fori_loop(0, query_block + 1, statistics, initial)
        log_total = maxima + jnp.log(totals)

        def mixing(key_block, accumulated):
            scores, admitted = block_scores(query_block, key_block)
            weights = jnp.where(admitted, jnp.exp(scores - log_total[:, None]), 0.0).astype(jnp.bfloat16)
            value_part = lax.dynamic_slice_in_dim(value_rows, key_block * block_rows, block_rows)
            return accumulated + jnp.dot(weights.astype(jnp.float32), value_part.astype(jnp.float32), preferred_element_type=jnp.float32)
        accumulated = lax.fori_loop(0, query_block + 1, mixing, jnp.zeros((span_rows, DH), jnp.float32))
        return (accumulated.astype(jnp.bfloat16), log_total)
    outputs, log_totals = lax.map(forward, jnp.arange(block_count, dtype=jnp.int32))
    out_rows = outputs.reshape(TOKENS * heads, DH)
    log_totals = log_totals.reshape(TOKENS * heads)
    dstat_rows = lax.optimization_barrier(jnp.sum(grad_rows.astype(jnp.float32) * out_rows.astype(jnp.float32), 1))

    def block_grads(query_block, key_block):
        scores, admitted = block_scores(query_block, key_block)
        log_block = lax.dynamic_slice_in_dim(log_totals, query_block * span_rows, span_rows)
        dstat_block = lax.dynamic_slice_in_dim(dstat_rows, query_block * span_rows, span_rows)
        grad_part = lax.dynamic_slice_in_dim(grad_rows, query_block * span_rows, span_rows)
        value_part = lax.dynamic_slice_in_dim(value_rows, key_block * block_rows, block_rows)
        prob_rows = jnp.where(admitted, jnp.exp(scores - log_block[:, None]), 0.0)
        dprobs = jnp.dot(grad_part.astype(jnp.float32), value_part.astype(jnp.float32).T, preferred_element_type=jnp.float32)
        dscores = (prob_rows * (dprobs - dstat_block[:, None]) * scaling).astype(jnp.bfloat16)
        return (prob_rows.astype(jnp.bfloat16), dscores, grad_part)

    def query_grad(query_block):

        def adding(key_block, accumulated):
            prob_rows, dscores, grad_part = block_grads(query_block, key_block)
            key_part = lax.dynamic_slice_in_dim(key_rows, key_block * block_rows, block_rows)
            return accumulated + jnp.dot(dscores.astype(jnp.float32), key_part.astype(jnp.float32), preferred_element_type=jnp.float32)
        accumulated = lax.fori_loop(0, query_block + 1, adding, jnp.zeros((span_rows, DH), jnp.float32))
        return accumulated.astype(jnp.bfloat16)

    def key_grad(key_block):

        def adding(query_block, accumulated):
            prob_rows, dscores, grad_part = block_grads(query_block, key_block)
            query_part = lax.dynamic_slice_in_dim(query_rows, query_block * span_rows, span_rows)
            dkey_part = jnp.dot(dscores.astype(jnp.float32).T, query_part.astype(jnp.float32), preferred_element_type=jnp.float32)
            dvalues = jnp.dot(prob_rows.astype(jnp.float32).T, grad_part.astype(jnp.float32), preferred_element_type=jnp.float32)
            return accumulated + jnp.concatenate([dkey_part, dvalues], 1)
        accumulated = lax.fori_loop(key_block, block_count, adding, jnp.zeros((block_rows, 2 * DH), jnp.float32))
        return accumulated.astype(jnp.bfloat16)
    dquery = lax.map(query_grad, jnp.arange(block_count, dtype=jnp.int32))
    dkv_rows = lax.map(key_grad, jnp.arange(block_count, dtype=jnp.int32))
    return (out_rows, dquery, dkv_rows)

def reference(queries, keys_values, stretch_ids, d_out):
    inverse = jnp.zeros((STRETCHES,), jnp.int32).at[stretch_ids].set(jnp.arange(STRETCHES, dtype=jnp.int32))

    def to_sorted(matrix):
        col_count = matrix.shape[1]
        return matrix.reshape(STRETCHES, STRETCH, col_count)[inverse].reshape(TOKENS, col_count)

    def to_devices(matrix):
        col_count = matrix.shape[1]
        return matrix.reshape(STRETCHES, STRETCH, col_count)[stretch_ids].reshape(TOKENS, col_count)
    group_heads = 2 * H
    query_sorted = to_sorted(queries)
    grad_sorted = to_sorted(d_out)
    pair_sorted = to_sorted(keys_values)

    def one_group(group_index):
        query_cols = lax.dynamic_slice_in_dim(query_sorted, group_index * (group_heads * DH), group_heads * DH, 1)
        grad_cols = lax.dynamic_slice_in_dim(grad_sorted, group_index * (group_heads * DH), group_heads * DH, 1)
        pair_cols = lax.dynamic_slice_in_dim(pair_sorted, group_index * (2 * DH), 2 * DH, 1)
        out_rows, dquery, dkv_rows = attend(query_cols.reshape(TOKENS * group_heads, DH), grad_cols.reshape(TOKENS * group_heads, DH), pair_cols[:, :DH], pair_cols[:, DH:], group_heads)
        return (out_rows.reshape(TOKENS, group_heads * DH), dquery.reshape(TOKENS, group_heads * DH), dkv_rows.reshape(TOKENS, 2 * DH))
    outputs, dqueries, dpairs = lax.map(one_group, jnp.arange(KVHEADS, dtype=jnp.int32))
    attn_out = jnp.transpose(outputs, (1, 0, 2)).reshape(TOKENS, QHEADS * DH)
    d_query = jnp.transpose(dqueries, (1, 0, 2)).reshape(TOKENS, QHEADS * DH)
    d_keys_values = jnp.transpose(dpairs, (1, 0, 2)).reshape(TOKENS, 2 * KVHEADS * DH)
    return (to_devices(attn_out), to_devices(d_query), to_devices(d_keys_values))
```

```python
import functools
import math

import jax
import jax.numpy as jnp
from jax import lax
from jax.experimental import pallas as pl
from jax.experimental.pallas import tpu as pltpu
from jax.sharding import PartitionSpec as P

T = 192
D = 128
HEADS = 4
ROWS = T * HEADS
STEP = 2 * T
SCALE = D**-0.5
LOG2E = math.log2(math.e)
LIMIT = 2.0**40
BLOCK = 2 * T
PIECE = 2 * BLOCK
TAGGED = BLOCK + 16
F32 = jnp.float32
BF16 = jnp.bfloat16


def dot(a, b):
    return jnp.dot(a, b, preferred_element_type=F32)


def steps_of(units):
    size = T * len(units)
    return [slice(at, min(at + STEP, size)) for at in range(0, size, STEP)]


def head_rows(ref, half):
    return jnp.concatenate(
        [ref[half * T : (half + 1) * T, n * D : (n + 1) * D] for n in range(HEADS)], 0
    )


def store_head_rows(ref, half, rows):
    for n in range(HEADS):
        ref[half * T : (half + 1) * T, n * D : (n + 1) * D] = rows[n * T : (n + 1) * T].astype(
            ref.dtype
        )


def read_tags(ref):
    packed = 0.0
    for block in range(2):
        tag = ref[block * TAGGED + BLOCK : (block + 1) * TAGGED].astype(F32)
        for u in range(2):
            packed = packed + tag[8 * u : 8 * u + 8] * float(64 ** (2 * block + u))
    code = jnp.max(packed).astype(jnp.int32)
    return [(code >> (6 * u)) & 31 for u in range(4)], (code >> 5) & 1


def admitted_list(ids, own, lst):
    found = jnp.int32(0)
    for n, stretch in enumerate(ids):
        lst[found] = jnp.int32(n)
        found = found + (stretch < own).astype(jnp.int32)
    return found


def over_groups(n, lst, body):
    at = 0
    for size in (4, 2, 1):
        groups = (n - at) // size

        def step(g, carry, size=size, at=at):
            body([lst[at + g * size + u] for u in range(size)])
            return carry

        lax.fori_loop(0, groups, step, 0)
        at = at + groups * size


def stack(ref, which, units):
    parts = [ref[which, rows_of(u), :] for u in units]
    return parts[0] if len(parts) == 1 else jnp.concatenate(parts, 0)


def values_and_ones(values):
    return jnp.concatenate([values.T, jnp.ones((16, values.shape[0]), BF16)], 0)


def causal_mask():
    key = lax.broadcasted_iota(jnp.int32, (T, ROWS), 0)
    row = lax.rem(lax.broadcasted_iota(jnp.int32, (T, ROWS), 1), T)
    return key <= row


def load_pairs(parity, mine, other, kv, first_row=0, size=PIECE):
    at = 0
    for a, b in zip(mine, other):
        for block in range(first_row // BLOCK, (first_row + size) // BLOCK):
            rows = slice(block * TAGGED, block * TAGGED + BLOCK)
            kv[parity, at : at + BLOCK] = a[rows]
            kv[1 - parity, at : at + BLOCK] = b[rows]
            at += BLOCK


def rows_of(unit):
    return pl.ds(pl.multiple_of(unit * T, 64), T)


def prep_kernel(q_ref, do_ref, qt, dt):
    for h in range(2):
        qt[h] = head_rows(q_ref, h).T
        dt[h] = head_rows(do_ref, h).T


def fwd_kernel(pieces, first, last, own_piece, qt, *refs):
    refs = list(refs)
    mine = refs[:pieces]
    other = refs[pieces : 2 * pieces]
    refs = refs[2 * pieces :]
    if not first:
        m_in, acc_in = refs[:2]
        refs = refs[2:]
    if last:
        dt = refs.pop(0)
    m, weights = refs[:2]
    refs = refs[2:]
    if last:
        out_ref, lse_ref, dstat_ref = refs[:3]
        refs = refs[3:]
    acc = refs[0]
    refs = refs[1:]
    kv, lst = refs
    own, parity = read_tags(own_piece)
    ids = [stretch for ref in mine for stretch in read_tags(ref)[0]]
    load_pairs(parity, mine, other, kv)

    def own_id(h):
        return jnp.where(h == 0, own[0], own[1])

    def start(h):
        if not first:
            m[h] = m_in[h]
            acc[h] = acc_in[h]
            return
        k = kv[0, rows_of(h), :]
        vt = values_and_ones(kv[1, rows_of(h), :])
        s = jnp.where(causal_mask(), dot(k, qt[h]), -1e30)
        top = jnp.max(s, 0, keepdims=True)
        p = jnp.exp2((s - top) * (SCALE * LOG2E))
        m[h] = top
        p = p.astype(BF16)
        weights[h, rows_of(h), :] = p
        acc[h] = dot(vt, p)

    def add_units(h, units):
        k = stack(kv, 0, units)
        vt = values_and_ones(stack(kv, 1, units))
        low = m[h] * (SCALE * LOG2E)
        steps = steps_of(units)
        later = dot(k[steps[0]], qt[h])
        part = 0.0
        for n, ks in enumerate(steps):
            s = later
            if n + 1 < len(steps):
                later = dot(k[steps[n + 1]], qt[h])
            p = jnp.exp2(s * (SCALE * LOG2E) - low).astype(BF16)
            for u in range(ks.start // T, ks.stop // T):
                weights[h, rows_of(units[u]), :] = p[u * T - ks.start : (u + 1) * T - ks.start]
            part += dot(vt[:, ks], p)
        acc[h] += part

    def half(h, carry):
        start(h)
        n = admitted_list(ids, own_id(h), lst)
        over_groups(n, lst, functools.partial(add_units, h))
        return carry

    def careful_half(h, carry):
        start(h)
        n = admitted_list(ids, own_id(h), lst)

        def highest(j, top):
            s = dot(kv[0, rows_of(lst[j]), :], qt[h])
            return jnp.maximum(top, jnp.max(s, 0, keepdims=True))

        top = lax.fori_loop(0, n, highest, m[h])
        alpha = jnp.exp2((m[h] - top) * (SCALE * LOG2E))
        m[h] = top
        acc[h] *= alpha
        if first:
            own_weights = weights[h, rows_of(h), :].astype(F32)
            weights[h, rows_of(h), :] = (own_weights * alpha).astype(BF16)

        def unit(j, c):
            add_units(h, [lst[j]])
            return c

        lax.fori_loop(0, n, unit, 0)
        return carry

    lax.fori_loop(0, 2, half, 0)

    @pl.when(jnp.max(jnp.maximum(acc[0, D : D + 1], acc[1, D : D + 1])) > LIMIT)
    def _():
        lax.fori_loop(0, 2, careful_half, 0)

    if last:
        for h in range(2):
            den = acc[h, D : D + 1]
            ot = (acc[h, :D] / den).astype(BF16).astype(F32)
            store_head_rows(out_ref, h, ot.T)
            dstat_ref[h] = jnp.sum(ot * dt[h].astype(F32), 0, keepdims=True)
            lse_ref[h] = m[h] * (SCALE * LOG2E) + jnp.log2(den)


def bwd_kernel(pieces, first_row, size, first, last, own_piece, m, weights, *refs):
    qt, dt, lse, dstat, *refs = refs
    mine = refs[:pieces]
    other = refs[pieces : 2 * pieces]
    refs = refs[2 * pieces :]
    if not first:
        dq_in = refs.pop(0)
    dq_out, *gm = refs[: 1 + pieces]
    go = refs[1 + pieces]
    refs = refs[2 + pieces :]
    dqt = refs.pop(0) if last else dq_out
    kv, g, qr, dr, factor, lst = refs
    first_unit = first_row // T
    for h in range(2):
        factor[h] = jnp.exp2(m[h] * (SCALE * LOG2E) - lse[h])
        qr[h] = (qt[h].astype(F32) * factor[h]).astype(BF16).T
        dr[h] = (dt[h].astype(F32) * factor[h]).astype(BF16).T
    if first:
        dqt[...] = jnp.zeros(dqt.shape, F32)
    else:
        dqt[...] = dq_in[...]
    g[...] = jnp.zeros(g.shape, F32)
    own, parity = read_tags(own_piece)
    ids = [stretch for ref in mine for stretch in read_tags(ref)[0]]
    ids = ids[first_unit : first_unit + pieces * size // T]
    load_pairs(parity, mine, other, kv, first_row, size)

    def half(h, carry):
        def body(units):
            v = stack(kv, 1, units)
            kt = stack(kv, 0, units).T
            p = stack(weights, h, [first_unit + u for u in units])
            steps = steps_of(units)
            later = dot(v[steps[0]], dt[h])
            dq = 0.0
            dk, dv = [], []
            for n, ks in enumerate(steps):
                dp = later
                if n + 1 < len(steps):
                    later = dot(v[steps[n + 1]], dt[h])
                dsc = (p[ks].astype(F32) * (dp - dstat[h])).astype(BF16)
                dq += dot(kt[:, ks], dsc)
                dk.append(dot(dsc, qr[h]))
                dv.append(dot(p[ks], dr[h]))
            dqt[h] += dq * factor[h]
            dk, dv = jnp.concatenate(dk, 0), jnp.concatenate(dv, 0)
            for u, unit in enumerate(units):
                g[0, rows_of(unit), :] += dk[u * T : (u + 1) * T]
                g[1, rows_of(unit), :] += dv[u * T : (u + 1) * T]

        if last:
            body([h])
        n = admitted_list(ids, jnp.where(h == 0, own[0], own[1]), lst)
        over_groups(n, lst, body)
        return carry

    lax.fori_loop(0, 2, half, 0)
    key_scale = jnp.where(parity == 0, SCALE, 1.0).astype(F32)
    other_scale = jnp.where(parity == 0, 1.0, SCALE).astype(F32)
    for n in range(pieces):
        gm[n][...] = (g[parity, n * size : (n + 1) * size] * key_scale).astype(gm[n].dtype)
    go[...] = (g[1 - parity] * other_scale).astype(BF16)
    if last:
        for h in range(2):
            store_head_rows(dq_out, h, dqt[h].T * SCALE)


VMEM = pl.BlockSpec(memory_space=pltpu.VMEM)
STAT = jax.ShapeDtypeStruct((2, 1, ROWS), F32)
ACC = jax.ShapeDtypeStruct((2, D, ROWS), F32)
ACC_AND_SUM = jax.ShapeDtypeStruct((2, D + 16, ROWS), F32)
BY_ROW = jax.ShapeDtypeStruct((2, ROWS, D), BF16)
BY_COL = jax.ShapeDtypeStruct((2, D, ROWS), BF16)


def vmem_of(shape):
    return pltpu.VMEM(shape.shape, shape.dtype)


def params():
    return pltpu.CompilerParams(vmem_limit_bytes=28 * 2**20)


def cost(products, keys):
    return pl.CostEstimate(
        flops=products * 2 * 2 * ROWS * keys * D,
        bytes_accessed=keys * 1024 + 2**21,
        transcendentals=2 * ROWS * keys,
    )


def prepare(q, do):
    return pl.pallas_call(
        prep_kernel,
        out_shape=[BY_COL, BY_COL],
        in_specs=[VMEM] * 2,
        out_specs=[VMEM] * 2,
        compiler_params=params(),
        name="prep",
    )(q, do)


def forward(own, qt, mine, other, state, dt=None):
    pieces = len(mine)
    first = state is None
    last = dt is not None
    out = jax.ShapeDtypeStruct((BLOCK, HEADS * D), BF16)
    args = [qt, *mine, *other] + ([] if first else list(state)) + ([dt] if last else [])
    return pl.pallas_call(
        functools.partial(fwd_kernel, pieces, first, last),
        out_shape=[
            STAT,
            jax.ShapeDtypeStruct((2, pieces * PIECE, ROWS), BF16),
        ]
        + ([out, STAT, STAT] if last else [ACC_AND_SUM]),
        in_specs=[VMEM] * (2 + 2 * pieces + (0 if first else 2) + (1 if last else 0)),
        out_specs=[VMEM] * (5 if last else 3),
        scratch_shapes=([vmem_of(ACC_AND_SUM)] if last else [])
        + [
            pltpu.VMEM((2, pieces * PIECE, D), BF16),
            pltpu.SMEM((4 * pieces + 1,), jnp.int32),
        ],
        compiler_params=params(),
        cost_estimate=cost(2, pieces * PIECE),
        name="fwd",
    )(own, *args)


def backward(own, kept, rows, mine, other, dqt, last=False, first_row=0, size=PIECE, kind=F32):
    pieces = len(mine)
    keys = pieces * size
    first = dqt is None
    out = jax.ShapeDtypeStruct((BLOCK, HEADS * D), BF16)
    args = [*kept, *rows, *mine, *other] + ([] if first else [dqt])
    return pl.pallas_call(
        functools.partial(bwd_kernel, pieces, first_row, size, first, last),
        out_shape=[
            out if last else ACC,
            *[jax.ShapeDtypeStruct((size, D), kind)] * pieces,
            jax.ShapeDtypeStruct((keys, D), BF16),
        ],
        in_specs=[VMEM] * (7 + 2 * pieces + (0 if first else 1)),
        out_specs=[VMEM] * (2 + pieces),
        scratch_shapes=([vmem_of(ACC)] if last else [])
        + [
            pltpu.VMEM((2, keys, D), BF16),
            pltpu.VMEM((2, keys, D), F32),
            vmem_of(BY_ROW),
            vmem_of(BY_ROW),
            vmem_of(STAT),
            pltpu.SMEM((4 * pieces + 1,), jnp.int32),
        ],
        compiler_params=params(),
        cost_estimate=cost(4, keys),
        name="bwd",
    )(own, *args)


def swap_cores(x):
    return lax.ppermute(x, "outer", [(i, i ^ 1) for i in range(lax.axis_size("outer"))])


def swap_x(x):
    return lax.ppermute(x, "inner", [(i, i ^ 1) for i in range(lax.axis_size("inner"))])


def swap_x_and_cores(x):
    n = lax.axis_size("inner")
    devices = lax.axis_size("outer") * n
    return lax.ppermute(x, ("outer", "inner"), [(i, i ^ n ^ 1) for i in range(devices)])


def swap_z(x, side, across=False):
    n = lax.axis_size("inner")

    def partner(i):
        z, x_lo = i // 2, i % 2
        step = 1 if (z + side) % 2 == 0 else -1
        return (z + step) % (n // 2) * 2 + (1 - x_lo if across else x_lo)

    return lax.ppermute(x, "inner", [(i, partner(i)) for i in range(n)])


def added(x, *terms):
    for t in terms:
        x = x + t.astype(F32)
    return x


def after(x, *others):
    return lax.optimization_barrier((x, *others))[0]


def local(queries, keys_values, stretch_ids, d_out):
    parity = (lax.axis_index("outer") % 2).astype(jnp.int32)
    tag = (stretch_ids + 32 * parity).astype(BF16)
    tag = jnp.broadcast_to(tag[:, None, None], (2, 8, D)).reshape(TAGGED - BLOCK, D)
    own = jnp.concatenate([keys_values, tag], 0)

    def paired(a, b):
        return jnp.concatenate([a, b], 0)

    piece = paired(own, swap_x(own))
    qt, dt = prepare(queries, d_out)

    chunks = [[piece]]
    others = []
    state = None
    hop = [paired(swap_z(own, side), swap_z(own, side, across=True)) for side in range(2)]
    kept = []
    for d in range(5):
        ready = [after(p, qt) for p in chunks[d]] if d == 0 else chunks[d]
        others.append([swap_cores(p) for p in ready])
        if d in (1, 2):
            hop = [swap_z(chunks[d][1], 0), swap_z(chunks[d][0], 1)]
        elif d == 3:
            hop = [swap_z(chunks[d][1], 0)]
        m, weights, *state = forward(
            piece, qt, chunks[d], others[d], state, dt if d == 4 else None
        )
        kept.append((m, weights))
        state = [m, *state]
        if d < 4:
            chunks.append([after(p, m) for p in hop] if d else hop)
    _, attn_out, lse, dstat = state
    rows = (qt, dt, lse, dstat)

    dq = None
    for d in range(4, 0, -1):
        dq, *grads = backward(piece, kept[d], rows, chunks[d], others[d], dq)
        back = swap_cores(grads.pop())
        sums = [added(g, back[n * PIECE : (n + 1) * PIECE]) for n, g in enumerate(grads)]
        if d == 3:
            sums[1] = added(sums[1], sent[0])
        elif d < 3:
            sums = [added(sums[0], sent[1]), added(sums[1], sent[0])]
        if d > 1:
            sent = [swap_z(g.astype(BF16), side) for side, g in enumerate(sums)]
    dq, beside, back = backward(
        piece, kept[0], rows, chunks[0], others[0], dq, first_row=BLOCK, size=BLOCK, kind=BF16
    )
    leaving = [part.astype(BF16) for g in sums for part in (g[:BLOCK], g[BLOCK:])]
    dq, *leaving = lax.optimization_barrier((dq, *leaving))
    sent = [swap_z(g, n // 2, across=n % 2 == 1) for n, g in enumerate(leaving)]
    sent += [swap_x(beside), swap_x_and_cores(back)]
    dq, total, back = backward(
        piece, kept[0], rows, chunks[0], others[0], dq, last=True, size=BLOCK
    )
    sent = lax.optimization_barrier((total, *sent))[1:]
    d_kv = added(total, swap_cores(back), *sent).astype(BF16)
    return (attn_out, dq, d_kv)


def solution(mesh):
    placed = (P("inner", "outer"), P("inner", "outer"), P("inner"), P("inner", "outer"))
    return jax.shard_map(
        local,
        mesh=mesh,
        in_specs=placed,
        out_specs=(P("inner", "outer"), P("inner", "outer"), P("inner", "outer")),
        check_vma=False,
    )
```
